32 devices in a mesh: row: 8 (over y, x, core), col: 4 (over z).
Axes of the slice: x: 2, y: 2, z: 4, core: 2. Of those that a mesh axis runs over, the one named last changes fastest.
Arguments:
- inputs: bfloat16 [8192, 2048], P('row', 'col'), may hold values from -6 to 6
- segments: int32 [8, 1024], P('row'), may hold values from 0 to 7, never falling along the last dimension, each value on 1 to 256 neighbouring positions
- routes: int32 [8192, 4], P('row'), may hold values from 0 to 7, all different within a row
- gain_attn: float32 [2048], P('col'), may hold values from 0.5 to 1.5
- w_query: bfloat16 [2048, 2048], P('row', 'col'), may hold values from -0.125 to 0.125
- w_key: bfloat16 [2048, 2048], P('row', 'col'), may hold values from -0.125 to 0.125
- w_value: bfloat16 [2048, 2048], P('row', 'col'), may hold values from -0.125 to 0.125
- b_query: float32 [2048], P('col'), may hold values from -1.2 to 1.2
- b_key: float32 [2048], P('col'), may hold values from -1.2 to 1.2
- b_value: float32 [2048], P('col'), may hold values from -1.2 to 1.2
- w_out: bfloat16 [2048, 2048], P('col', 'row'), may hold values from -0.75 to 0.75
- gain_ffn: float32 [2048], P('col'), may hold values from 0.5 to 1.5
- w_router: bfloat16 [2048, 8], P('row'), may hold values from -0.0625 to 0.0625
- w_expert_gate: bfloat16 [8, 2048, 1408], P('col', 'row'), may hold values from -0.125 to 0.125
- w_expert_up: bfloat16 [8, 2048, 1408], P('col', 'row'), may hold values from -0.125 to 0.125
- w_expert_down: bfloat16 [8, 1408, 2048], P('col', None, 'row'), may hold values from -0.625 to 0.625
- w_shared_gate: bfloat16 [2048, 5632], P('row', 'col'), may hold values from -0.125 to 0.125
- w_shared_up: bfloat16 [2048, 5632], P('row', 'col'), may hold values from -0.125 to 0.125
- w_shared_down: bfloat16 [5632, 2048], P('col', 'row'), may hold values from -0.15625 to 0.15625
- w_shared_mix: bfloat16 [2048], P('row'), may hold values from -0.125 to 0.125
- cotangent: bfloat16 [8192, 2048], P('row', 'col'), may hold values from -6 to 6
Outputs:
- output: float32 [8192, 2048], P('row', 'col')
- input_grad: float32 [8192, 2048], P('row', 'col')
- grad_gain_attn: float32 [2048], P('col')
- grad_w_query: float32 [2048, 2048], P('row', 'col')
- grad_w_key: float32 [2048, 2048], P('row', 'col')
- grad_w_value: float32 [2048, 2048], P('row', 'col')
- grad_b_query: float32 [2048], P('col')
- grad_b_key: float32 [2048], P('col')
- grad_b_value: float32 [2048], P('col')
- grad_w_out: float32 [2048, 2048], P('col', 'row')
- grad_gain_ffn: float32 [2048], P('col')
- grad_w_router: float32 [2048, 8], P('row')
- grad_w_expert_gate: float32 [8, 2048, 1408], P('col', 'row')
- grad_w_expert_up: float32 [8, 2048, 1408], P('col', 'row')
- grad_w_expert_down: float32 [8, 1408, 2048], P('col', None, 'row')
- grad_w_shared_gate: float32 [2048, 5632], P('row', 'col')
- grad_w_shared_up: float32 [2048, 5632], P('row', 'col')
- grad_w_shared_down: float32 [5632, 2048], P('col', 'row')
- grad_w_shared_mix: float32 [2048], P('row')
The draws below stay inside these ranges and needn't reach their ends.
Inputs may be any that keep to these rules, and one draw needn't show every extreme that they name: `segments`: within each sequence of 1024 tokens the segment numbers never fall. `routes`: each token names 4 different experts.
All inputs are finite; a program needn't handle non-finite values.
Results may differ from the reference program's by a relative error of at most 0.033.
Values may be sent and summed in bfloat16 or wider, within the bound.
No kernel may reach another device: no remote copies, remote signals or barrier semaphores. Data moves between devices by JAX's collectives and lax.ppermute only.
A program may use at most 320 MiB of HBM per device.

```python
import math
import jax
import jax.numpy as jnp
import numpy as np
from jax import lax

D = 2048
HEADS = 16
HEAD_DIM = 128
FFE = 1408
FFS = 5632
EXPERTS = 8
TOP = 4
TOK_DEV = 1024
HID = 2048
CAP = 576
SEQS = 8
TOKENS = 8192


def steps_of(key, shape, pieces, least, largest):
    level, own = 1.0, jax.random.fold_in(key, 6)
    for dim, blocks in pieces:
        draws = jnp.exp(jax.random.uniform(jax.random.fold_in(own, dim), (blocks,), jnp.float32, least / len(pieces), largest / len(pieces)))
        level = level * jnp.repeat(draws, shape[dim] // blocks).reshape([-1 if axis == dim else 1 for axis in range(len(shape))])
    return level


def different_ones(stream_key, rows, amount, top, lift):
    order = jax.random.permutation(jax.random.fold_in(stream_key, 1), amount)
    favour = order
    for power in range(3):
        favour = favour * favour // amount
    favour = favour * lift // amount
    chance = jax.random.randint(jax.random.fold_in(stream_key, 2), (rows, amount), 0, 4096) + favour
    sure = jax.random.permutation(jax.random.fold_in(stream_key, 3), rows)[jnp.arange(amount) % rows]
    chance = jnp.where(jnp.arange(rows)[:, None] == sure[None, :], 1 << 14, chance)
    priority = chance * amount + jnp.arange(amount)
    return lax.top_k(priority.astype(jnp.int32), top)[1].astype(jnp.int32)


def length_profile(count, total, most, slope):
    portions = [(1 << 20) // math.isqrt(grade ** slope) + 1 for grade in range(2, count + 1)]
    spare, counts = total - most - (count - 1), [1] * (count - 1)
    while spare > 0:
        movable = [i for i in range(count - 1) if counts[i] < most]
        pool, remaining = sum([portions[i] for i in movable]), spare
        for i in movable:
            more = min(most - counts[i], max(1, remaining * portions[i] // pool), spare)
            counts[i] = counts[i] + more
            spare = spare - more
    return np.array([most] + counts)


def uneven_parts(rng, number_of, total, bound, slope):
    if number_of == 2:
        one = jax.random.randint(rng, (), max(1, total - bound), min(bound, total - 1) + 1)
        return jnp.stack([one, total - one])
    sizes = jnp.asarray(length_profile(number_of, total, bound, slope), jnp.int32)
    twos = (number_of - 1) // 2
    giver, receiver = sizes[1:1 + 2 * twos:2], sizes[2:2 + 2 * twos:2]
    slack = jnp.minimum(giver - 1, bound - receiver)
    moved = jax.random.randint(jax.random.fold_in(rng, 1), (twos,), 0, 1 << 20) % (slack + 1)
    sizes = sizes.at[1:1 + 2 * twos:2].set(giver - moved).at[2:2 + 2 * twos:2].set(receiver + moved)
    return sizes[jax.random.permutation(jax.random.fold_in(rng, 2), number_of)]


def centred(own_key, shape, spread, bound, shards=(), dtype=jnp.bfloat16):
    factor_of = steps_of(own_key, shape, shards, -0.22, 0.18) if shards else 1.0
    drawn = jax.random.normal(own_key, shape, jnp.float32) * spread * factor_of
    return jnp.minimum(jnp.maximum(drawn, -bound), bound).astype(dtype)


def setup_inputs(seed: int = 0) -> dict:
    key_of = jax.random.split(jax.random.key(seed), 22)
    return {
        "inputs": centred(key_of[0], (TOKENS, D), 1.0, 6.0, ((0, 8), (1, 4))),
        "segments": jax.vmap(lambda own: jnp.searchsorted(jnp.cumsum(uneven_parts(own, 8, TOK_DEV, TOK_DEV // 4, 1)), jnp.arange(TOK_DEV), side="right"))(jax.random.split(key_of[1], SEQS)).reshape((SEQS, TOK_DEV)).astype(jnp.int32),
        "routes": different_ones(key_of[2], TOKENS, EXPERTS, TOP, 4096),
        "gain_attn": jnp.clip(1.0 + 0.1 * jax.random.normal(key_of[3], (D,), jnp.float32), 0.5, 1.5),
        "w_query": centred(key_of[4], (D, HID), D ** -0.5, 0.125, ((0, 8), (1, 4))),
        "w_key": centred(key_of[5], (D, HID), D ** -0.5, 0.125, ((0, 8), (1, 4))),
        "w_value": centred(key_of[6], (D, HID), D ** -0.5, 0.125, ((0, 8), (1, 4))),
        "b_query": centred(key_of[7], (HID,), 0.2, 1.2, ((0, 4),), jnp.float32),
        "b_key": centred(key_of[8], (HID,), 0.2, 1.2, ((0, 4),), jnp.float32),
        "b_value": centred(key_of[9], (HID,), 0.2, 1.2, ((0, 4),), jnp.float32),
        "w_out": centred(key_of[10], (HID, D), (HID // 32) ** -0.5, 0.75, ((0, 4), (1, 8))),
        "gain_ffn": jnp.clip(1.0 + 0.1 * jax.random.normal(key_of[11], (D,), jnp.float32), 0.5, 1.5),
        "w_router": centred(key_of[12], (D, EXPERTS), (4 * D) ** -0.5, 0.0625, ((0, 8),)),
        "w_expert_gate": centred(key_of[13], (EXPERTS, D, FFE), D ** -0.5, 0.125, ((0, 4), (1, 8))),
        "w_expert_up": centred(key_of[14], (EXPERTS, D, FFE), D ** -0.5, 0.125, ((0, 4), (1, 8))),
        "w_expert_down": centred(key_of[15], (EXPERTS, FFE, D), (FFE // 16) ** -0.5, 0.625, ((0, 4), (2, 8))),
        "w_shared_gate": centred(key_of[16], (D, FFS), D ** -0.5, 0.125, ((0, 8), (1, 4))),
        "w_shared_up": centred(key_of[17], (D, FFS), D ** -0.5, 0.125, ((0, 8), (1, 4))),
        "w_shared_down": centred(key_of[18], (FFS, D), (FFS // 4) ** -0.5, 0.15625, ((0, 4), (1, 8))),
        "w_shared_mix": centred(key_of[19], (D,), D ** -0.5, 0.125, ((0, 8),)),
        "cotangent": centred(key_of[20], (TOKENS, D), 1.0, 6.0, ((0, 8), (1, 4))),
    }


EPSILON = 1e-06
THETA = 1000000.0
NEGATIVE = -1e+30

@jax.custom_vjp
def low(v):
    return lax.optimization_barrier(v.astype(jnp.bfloat16)).astype(jnp.float32)

@jax.custom_vjp
def low_back(v):
    return v

def low_keep(v):
    return (low(v), None)

def low_pass(kept, grad):
    return (grad,)

def back_keep(v):
    return (v, None)

def back_low(kept, grad):
    return (low(grad),)
low.defvjp(low_keep, low_pass)
low_back.defvjp(back_keep, back_low)

def matmul(left_side, right_side):
    return jnp.dot(left_side, right_side, precision=lax.Precision.HIGHEST)

def rms_norm(values, gain_vector):
    mean_square = lax.optimization_barrier(jnp.mean(values * values, axis=-1, keepdims=True))
    return values * lax.rsqrt(mean_square + EPSILON) * gain_vector

def rotary_tables(length):
    position = jnp.arange(length).astype(jnp.float32)
    exponent = jnp.arange(HEAD_DIM // 2).astype(jnp.float32) * (2.0 / HEAD_DIM)
    angles = position[:, None] * jnp.exp(-exponent * jnp.log(THETA))[None, :]
    return (jnp.cos(angles)[:, None, :], jnp.sin(angles)[:, None, :])

def rotate(values, cosine_table, sine_table):
    half_dim = values.shape[-1] // 2
    first_half = values[..., :half_dim]
    second_half = values[..., half_dim:]
    return jnp.concatenate([first_half * cosine_table - second_half * sine_table, second_half * cosine_table + first_half * sine_table], axis=-1)

def route_slots(routes_seq):
    flat_routes = routes_seq.reshape(-1)
    onehot = (flat_routes[:, None] == jnp.arange(EXPERTS)[None, :]).astype(jnp.int32)
    position_in = lax.optimization_barrier(jnp.sum(jnp.cumsum(onehot, axis=0) * onehot, axis=1)) - 1
    keep_pair = position_in < CAP
    slot_pair = jnp.where(keep_pair, flat_routes * CAP + position_in, EXPERTS * CAP).astype(jnp.int32)
    token_pair = (jnp.arange(flat_routes.shape[0]) // TOP).astype(jnp.int32)
    slot_token = jnp.zeros((EXPERTS * CAP,), jnp.int32).at[slot_pair].set(token_pair, mode='drop')
    slot_live = jnp.zeros((EXPERTS * CAP,), jnp.float32).at[slot_pair].set(1.0, mode='drop')
    safe_slot = jnp.minimum(slot_pair, EXPERTS * CAP - 1)
    return (slot_token, slot_live, safe_slot, keep_pair.astype(jnp.float32))

def layer_sequence(params, inputs_seq, segment_seq, routes_seq):
    gain_attn, w_query, w_key, w_value, b_query, b_key, b_value, w_out, gain_ffn, w_router, w_expert_gate, w_expert_up, w_expert_down, w_shared_gate, w_shared_up, w_shared_down, w_shared_mix = params
    highest = lax.Precision.HIGHEST
    length = inputs_seq.shape[0]
    normed = low(rms_norm(inputs_seq, gain_attn))
    cosine_table, sine_table = rotary_tables(length)
    query_pre = low_back(matmul(normed, w_query) + b_query).reshape(length, HEADS, HEAD_DIM)
    key_pre = low_back(matmul(normed, w_key) + b_key).reshape(length, HEADS, HEAD_DIM)
    value_heads = low(low_back(matmul(normed, w_value) + b_value)).reshape(length, HEADS, HEAD_DIM)
    query_rot = low(rotate(query_pre, cosine_table, sine_table))
    key_rot = low(rotate(key_pre, cosine_table, sine_table))
    logits = jnp.einsum('qhd,khd->hqk', query_rot, key_rot, precision=highest) * HEAD_DIM ** (-0.5)
    scores = low_back(logits)
    position = jnp.arange(length)
    allowed = (position[None, :] <= position[:, None]) & (segment_seq[None, :] == segment_seq[:, None])
    weights_soft = jax.nn.softmax(jnp.where(allowed[None], scores, NEGATIVE), axis=-1)
    mixed_heads = low(low_back(jnp.einsum('hqk,khd->qhd', low(weights_soft), value_heads, precision=highest))).reshape(length, HID)
    residual = inputs_seq + matmul(mixed_heads, w_out)
    normed_ffn = low(rms_norm(residual, gain_ffn))
    router_probs = jax.nn.softmax(matmul(normed_ffn, w_router), axis=-1)
    gate_pair = jnp.take_along_axis(router_probs, routes_seq, axis=1).reshape(-1)
    slot_token, slot_live, safe_slot, keep_pair = route_slots(routes_seq)
    buffer = (normed_ffn[slot_token] * slot_live[:, None]).reshape(EXPERTS, CAP, D)
    gate_part = low_back(jnp.einsum('ecd,edf->ecf', buffer, w_expert_gate, precision=highest))
    up_part = low_back(jnp.einsum('ecd,edf->ecf', buffer, w_expert_up, precision=highest))
    activated = low(jax.nn.silu(gate_part) * up_part)
    expert_out = low_back(jnp.einsum('ecf,efd->ecd', activated, w_expert_down, precision=highest)).reshape(EXPERTS * CAP, D)
    routed = lax.optimization_barrier(jnp.sum((expert_out[safe_slot] * (gate_pair * keep_pair)[:, None]).reshape(length, TOP, D), axis=1))
    shared_act = low(jax.nn.silu(low_back(matmul(normed_ffn, w_shared_gate))) * low_back(matmul(normed_ffn, w_shared_up)))
    mix_gate = jax.nn.sigmoid(matmul(normed_ffn, w_shared_mix))
    shared_out = mix_gate[:, None] * low_back(matmul(shared_act, w_shared_down))
    return residual + routed + shared_out

def reference(inputs, segments, routes, gain_attn, w_query, w_key, w_value, b_query, b_key, b_value, w_out, gain_ffn, w_router, w_expert_gate, w_expert_up, w_expert_down, w_shared_gate, w_shared_up, w_shared_down, w_shared_mix, cotangent):
    params = tuple((member.astype(jnp.float32) for member in (gain_attn, w_query, w_key, w_value, b_query, b_key, b_value, w_out, gain_ffn, w_router, w_expert_gate, w_expert_up, w_expert_down, w_shared_gate, w_shared_up, w_shared_down, w_shared_mix)))
    sequences = segments.shape[0]
    seq_inputs = inputs.astype(jnp.float32).reshape(sequences, TOK_DEV, D)
    seq_routes = routes.reshape(sequences, TOK_DEV, TOP)

    def forward(weights, seq_values):

        def one_sequence(members):
            return layer_sequence(weights, members[0], members[1], members[2])
        return lax.map(jax.checkpoint(one_sequence), (seq_values, segments, seq_routes))
    outputs, pullback = jax.vjp(forward, params, seq_inputs)
    grad_params, grad_inputs = pullback(cotangent.astype(jnp.float32).reshape(sequences, TOK_DEV, D))
    return (outputs.reshape(TOKENS, D), grad_inputs.reshape(TOKENS, D), grad_params[0], grad_params[1], grad_params[2], grad_params[3], grad_params[4], grad_params[5], grad_params[6], grad_params[7], grad_params[8], grad_params[9], grad_params[10], grad_params[11], grad_params[12], grad_params[13], grad_params[14], grad_params[15], grad_params[16])
```

```python
import functools

import jax
import jax.numpy as jnp
from jax import lax
from jax.experimental import pallas as pl
from jax.experimental.pallas import tpu as pltpu
from jax.sharding import PartitionSpec as P

HEAD_DIM = 128
EXPERTS = 8
TOP = 4
CAP = 576
SPAN = 256

EPSILON = 1e-06
THETA = 1000000.0
NEGATIVE = -1e30

f32 = jnp.float32
bf16 = jnp.bfloat16


def dot_nn(left, right):
    return jnp.dot(left, right, preferred_element_type=f32)


def dot_nt(left, right):
    return lax.dot_general(left, right, (((1,), (1,)), ((), ())), preferred_element_type=f32)


def dot_tn(left, right):
    return lax.dot_general(left, right, (((0,), (0,)), ((), ())), preferred_element_type=f32)


def batch_nn(left, right):
    return jnp.einsum("ecd,edf->ecf", left, right, preferred_element_type=f32)


def batch_nt(left, right):
    return jnp.einsum("ecf,edf->ecd", left, right, preferred_element_type=f32)


def batch_tn(left, right):
    return jnp.einsum("ecd,ecf->edf", left, right, preferred_element_type=f32)


def line_gather(block, count, me):
    width = block.shape[1]
    full = jnp.zeros((block.shape[0], count * width), block.dtype)
    full = lax.dynamic_update_slice_in_dim(full, block, me * width, 1)
    up = down = block
    for step in range(1, count):
        up = lax.ppermute(up, "col", [(i, i + 1) for i in range(step - 1, count - 1)])
        down = lax.ppermute(down, "col", [(i, i - 1) for i in range(1, count - step + 1)])
        from_below = me >= step
        from_above = me + step < count
        full = lax.dynamic_update_slice_in_dim(
            full, jnp.where(from_below, up, block), jnp.where(from_below, me - step, me) * width, 1
        )
        full = lax.dynamic_update_slice_in_dim(
            full, jnp.where(from_above, down, block), jnp.where(from_above, me + step, me) * width, 1
        )
    return full


def line_scatter(partial, count, me):
    width = partial.shape[1] // count

    def block(index):
        return lax.dynamic_slice_in_dim(partial, index * width, width, 1)

    up = down = None
    for far in range(count - 1, 0, -1):
        up_out, down_out = block(me + far), block(me - far)
        if up is not None:
            up_out = (up_out.astype(f32) + up.astype(f32)).astype(bf16)
            down_out = (down_out.astype(f32) + down.astype(f32)).astype(bf16)
        up = lax.ppermute(up_out, "col", [(i, i + 1) for i in range(count - far)])
        down = lax.ppermute(down_out, "col", [(i, i - 1) for i in range(far, count)])
    return block(me).astype(f32) + up.astype(f32) + down.astype(f32)


def all_of_col(block, count, me):
    full = jnp.zeros((count,) + block.shape, block.dtype)
    full = lax.dynamic_update_slice_in_dim(full, block[None], me, 0)
    for step in range(1, count):
        got = lax.ppermute(block, "col", [(i, (i + step) % count) for i in range(count)])
        full = lax.dynamic_update_slice_in_dim(full, got[None], lax.rem(me + count - step, count), 0)
    return full


def spans(length):
    return [(max(0, first - SPAN), first, first + SPAN) for first in range(0, length, SPAN)]


def turned(values, cosine, sine):
    return values * cosine + pltpu.roll(values, HEAD_DIM // 2, 1) * sine


def turned_back(values, cosine, sine):
    return values * cosine - pltpu.roll(values, HEAD_DIM // 2, 1) * sine


def soft_weights(query, key, seg_col, seg_row, low, first, high):
    scores = dot_nt(query, key) * HEAD_DIM ** (-0.5)
    shape = (high - first, high - low)
    at_query = first + lax.broadcasted_iota(jnp.int32, shape, 0)
    at_key = low + lax.broadcasted_iota(jnp.int32, shape, 1)
    allowed = (at_key <= at_query) & (seg_col[first:high, :] == seg_row[:, low:high])
    scores = jnp.where(allowed, scores, NEGATIVE)
    weights = jnp.exp(scores - jnp.max(scores, axis=1, keepdims=True))
    return weights / jnp.sum(weights, axis=1, keepdims=True)


def attend_kernel(pre, bias, cosine, sine, seg_col, seg_row, mixed, turned_out):
    length = pre.shape[0]
    d = HEAD_DIM
    pre_q = pre[:, :d] + bias[:, :d]
    pre_k = pre[:, d : 2 * d] + bias[:, d : 2 * d]
    turned_out[:, :d] = turned(pre_q, cosine[...], sine[...]).astype(bf16)
    turned_out[:, d : 2 * d] = turned(pre_k, cosine[...], sine[...]).astype(bf16)
    turned_out[:, 2 * d :] = (pre[:, 2 * d :] + bias[:, 2 * d :]).astype(bf16)
    for low, first, high in spans(length):
        weights = soft_weights(
            turned_out[first:high, :d], turned_out[low:high, d : 2 * d], seg_col, seg_row, low, first, high
        )
        mixed[first:high, :] = dot_nn(weights.astype(bf16), turned_out[low:high, 2 * d :]).astype(bf16)


def attend_back_kernel(heads, cosine, sine, seg_col, seg_row, grad_mixed, grad_pre, grad_bias, key_sum, value_sum):
    length = heads.shape[0]
    d = HEAD_DIM
    scale = d ** (-0.5)
    key_sum[...] = jnp.zeros_like(key_sum)
    value_sum[...] = jnp.zeros_like(value_sum)
    query_bias = jnp.zeros((1, d), f32)
    for low, first, high in spans(length):
        query, key, value = heads[first:high, :d], heads[low:high, d : 2 * d], heads[low:high, 2 * d :]
        grad = grad_mixed[first:high, :]
        weights = soft_weights(query, key, seg_col, seg_row, low, first, high)
        grad_soft = dot_nt(grad, value)
        inner = jnp.sum(weights * grad_soft, axis=1, keepdims=True)
        grad_scores = (weights * (grad_soft - inner)).astype(bf16)
        grad_query = dot_nn(grad_scores, key) * scale
        grad_query = turned_back(grad_query, cosine[first:high, :], sine[first:high, :]).astype(bf16)
        grad_pre[first:high, :d] = grad_query
        query_bias += jnp.sum(grad_query.astype(f32), axis=0, keepdims=True)
        key_sum[low:high, :] += dot_tn(grad_scores, query) * scale
        value_sum[low:high, :] += dot_tn(weights.astype(bf16), grad)
    grad_key = turned_back(key_sum[...], cosine[...], sine[...]).astype(bf16)
    grad_value = value_sum[...].astype(bf16)
    grad_pre[:, d : 2 * d] = grad_key
    grad_pre[:, 2 * d :] = grad_value
    grad_bias[:, :d] = query_bias
    grad_bias[:, d : 2 * d] = jnp.sum(grad_key.astype(f32), axis=0, keepdims=True)
    grad_bias[:, 2 * d :] = jnp.sum(grad_value.astype(f32), axis=0, keepdims=True)


def head_spec(rows, width):
    return pl.BlockSpec((rows, width), lambda h: (0, h))


def whole_spec(array):
    return pl.BlockSpec(array.shape, lambda h: (0, 0))


def attend(pre, bias, cosine, sine, seg_col, seg_row):
    length, width = pre.shape
    heads = width // (3 * HEAD_DIM)
    return pl.pallas_call(
        attend_kernel,
        grid=(heads,),
        in_specs=[
            head_spec(length, 3 * HEAD_DIM),
            head_spec(1, 3 * HEAD_DIM),
            whole_spec(cosine),
            whole_spec(sine),
            whole_spec(seg_col),
            whole_spec(seg_row),
        ],
        out_specs=[head_spec(length, HEAD_DIM), head_spec(length, 3 * HEAD_DIM)],
        out_shape=[
            jax.ShapeDtypeStruct((length, heads * HEAD_DIM), bf16),
            jax.ShapeDtypeStruct((length, width), bf16),
        ],
        compiler_params=pltpu.CompilerParams(vmem_limit_bytes=32 << 20),
        cost_estimate=pl.CostEstimate(
            flops=heads * length * 2 * SPAN * HEAD_DIM * 4, bytes_accessed=10 * length * width, transcendentals=0
        ),
    )(pre, bias, cosine, sine, seg_col, seg_row)


def attend_back(heads_pre, cosine, sine, seg_col, seg_row, grad_mixed):
    length, width = heads_pre.shape
    heads = width // (3 * HEAD_DIM)
    return pl.pallas_call(
        attend_back_kernel,
        grid=(heads,),
        in_specs=[
            head_spec(length, 3 * HEAD_DIM),
            whole_spec(cosine),
            whole_spec(sine),
            whole_spec(seg_col),
            whole_spec(seg_row),
            head_spec(length, HEAD_DIM),
        ],
        out_specs=[head_spec(length, 3 * HEAD_DIM), head_spec(1, 3 * HEAD_DIM)],
        out_shape=[
            jax.ShapeDtypeStruct((length, width), bf16),
            jax.ShapeDtypeStruct((1, width), f32),
        ],
        scratch_shapes=[pltpu.VMEM((length, HEAD_DIM), f32), pltpu.VMEM((length, HEAD_DIM), f32)],
        compiler_params=pltpu.CompilerParams(vmem_limit_bytes=32 << 20),
        cost_estimate=pl.CostEstimate(
            flops=heads * length * 2 * SPAN * HEAD_DIM * 10, bytes_accessed=8 * length * width, transcendentals=0
        ),
    )(heads_pre, cosine, sine, seg_col, seg_row, grad_mixed)


def rotary_tables(length):
    position = jnp.arange(length).astype(f32)
    exponent = jnp.arange(HEAD_DIM // 2).astype(f32) * (2.0 / HEAD_DIM)
    angles = position[:, None] * jnp.exp(-exponent * jnp.log(THETA))[None, :]
    cosine, sine = jnp.cos(angles), jnp.sin(angles)
    return jnp.concatenate([cosine, cosine], 1), jnp.concatenate([-sine, sine], 1)


def by_head(parts):
    rows = parts[0].shape[0]
    split = [part.reshape(rows, -1, 1, HEAD_DIM) for part in parts]
    return jnp.concatenate(split, axis=2).reshape(rows, -1)


def from_heads(joined):
    split = joined.reshape(joined.shape[0], -1, 3, HEAD_DIM)
    return [split[:, :, i].reshape(joined.shape[0], -1) for i in range(3)]


def two_terms(values):
    high = values.astype(bf16)
    return high, (values - high.astype(f32)).astype(bf16)


def local(
    rows,
    cols,
    inputs,
    segments,
    routes,
    gain_attn,
    w_query,
    w_key,
    w_value,
    b_query,
    b_key,
    b_value,
    w_out,
    gain_ffn,
    w_router,
    w_expert_gate,
    w_expert_up,
    w_expert_down,
    w_shared_gate,
    w_shared_up,
    w_shared_down,
    w_shared_mix,
    cotangent,
):
    length, part = inputs.shape
    width = part * cols
    experts, depth, hidden = w_expert_gate.shape
    hidden_shared = w_shared_gate.shape[1]
    head_width = w_query.shape[1]
    alike = hidden == hidden_shared
    col = lax.axis_index("col")
    row = lax.axis_index("row")

    def mine(array, axis=1):
        return lax.dynamic_slice_in_dim(array, col * part, part, axis)

    all_heads = lax.all_gather(by_head([w_query, w_key, w_value]), "row", axis=0, tiled=True)
    out_rows = line_gather(w_out.T, cols, col).T
    all_out = lax.all_gather(out_rows, "row", axis=1, tiled=True)
    expert_in = jnp.concatenate([w_expert_gate, w_expert_up], axis=2)
    shared_in = jnp.concatenate([w_shared_gate, w_shared_up], axis=1)[None]
    shared_down = w_shared_down[None]
    if alike:
        all_in = lax.all_gather(jnp.concatenate([expert_in, shared_in], 0), "row", axis=1, tiled=True)
        all_down = lax.all_gather(jnp.concatenate([w_expert_down, shared_down], 0), "row", axis=2, tiled=True)
        expert_in, shared_in = all_in[:experts], all_in[experts]
        expert_down, shared_down = all_down[:experts], all_down[experts]
    else:
        expert_in = lax.all_gather(expert_in, "row", axis=1, tiled=True)
        shared_in = lax.all_gather(shared_in, "row", axis=1, tiled=True)[0]
        expert_down = lax.all_gather(w_expert_down, "row", axis=2, tiled=True)
        shared_down = lax.all_gather(shared_down, "row", axis=2, tiled=True)[0]
    w_small = jnp.concatenate([w_router, w_shared_mix[:, None]], 1)
    all_small = lax.all_gather(w_small, "row", axis=0, tiled=True)
    gains = lax.all_gather(jnp.stack([gain_attn, gain_ffn]), "col", axis=1, tiled=True)

    named = jnp.any(routes[:, :, None] == jnp.arange(EXPERTS)[None, None, :], axis=1)
    at = jnp.arange(length)
    earlier = (at[None, :] < at[:, None]).astype(bf16)
    place = dot_nn(earlier, named.astype(bf16))
    kept = named & (place < CAP)
    place_here = lax.dynamic_slice_in_dim(jnp.where(kept, place, -1.0), col * experts, experts, 1)
    slots = (place_here[:, :, None] == jnp.arange(CAP).astype(f32)[None, None, :]).astype(bf16)
    slots = slots.reshape(length, experts * CAP)

    cosine, sine = rotary_tables(length)
    seg_row = segments
    seg_col = segments.T

    inputs_full = line_gather(inputs, cols, col)
    inputs_wide = inputs_full.astype(f32)
    inverse_attn = lax.rsqrt(jnp.mean(inputs_wide * inputs_wide, axis=1, keepdims=True) + EPSILON)
    normed = (inputs_wide * inverse_attn * gains[0][None, :]).astype(bf16)
    bias = by_head([b_query[None], b_key[None], b_value[None]])
    mixed, heads_pre = attend(dot_nn(normed, all_heads), bias, cosine, sine, seg_col, seg_row)
    mixed_full = line_gather(mixed, cols, col)
    residual = inputs_wide + dot_nn(mixed_full, all_out)
    inverse_ffn = lax.rsqrt(jnp.mean(residual * residual, axis=1, keepdims=True) + EPSILON)
    normed_ffn = (residual * inverse_ffn * gains[1][None, :]).astype(bf16)
    residual_mine = mine(residual)

    cotangent_full = line_gather(cotangent, cols, col)

    logits = dot_nn(normed_ffn, all_small)
    probs = jax.nn.softmax(logits[:, :EXPERTS], axis=-1)
    mix_gate = jax.nn.sigmoid(logits[:, EXPERTS:])
    probs_here = lax.dynamic_slice_in_dim(probs, col * experts, experts, 1)
    slot_gates = sum(dot_tn(slots, term) for term in two_terms(probs_here))
    slot_gate = jnp.concatenate(
        [slot_gates[e * CAP : (e + 1) * CAP, e : e + 1][None] for e in range(experts)], axis=0
    )

    buffer = dot_tn(slots, normed_ffn).astype(bf16).reshape(experts, CAP, width)
    expert_pre = batch_nn(buffer, expert_in).astype(bf16)
    shared_pre = dot_nn(normed_ffn, shared_in).astype(bf16)

    def halves(pre):
        half = pre.shape[-1] // 2
        return pre[..., :half].astype(f32), pre[..., half:].astype(f32)

    def activated(pre, scale):
        gate, up = halves(pre)
        return (gate * jax.nn.sigmoid(gate) * up * scale).astype(bf16)

    expert_act = activated(expert_pre, slot_gate)
    shared_act = activated(shared_pre, mix_gate)
    cotangent_slot = dot_tn(slots, cotangent_full).astype(bf16).reshape(experts, CAP, width)
    grad_expert_down = batch_tn(expert_act, cotangent_slot).astype(bf16)
    grad_shared_down = dot_tn(shared_act, cotangent_full).astype(bf16)[None]
    expert_out = batch_nn(expert_act, expert_down).astype(bf16).reshape(experts * CAP, width)
    ffn_partial = (dot_nn(slots, expert_out) + dot_nn(shared_act, shared_down)).astype(bf16)
    output = residual_mine + line_scatter(ffn_partial, cols, col)

    def pre_back(pre, grad_act, scale):
        gate, up = halves(pre)
        sigmoid = jax.nn.sigmoid(gate)
        silu = gate * sigmoid
        dots = jnp.sum(silu * up * grad_act, axis=-1)
        scaled = grad_act * scale
        grad_gate = scaled * up * sigmoid * (1.0 + gate * (1.0 - sigmoid))
        grad_up = scaled * silu
        stat = jnp.sum(grad_gate * gate + grad_up * up, axis=-1)
        return jnp.concatenate([grad_gate.astype(bf16), grad_up.astype(bf16)], axis=-1), dots, stat

    grad_expert_pre, expert_dots, expert_stat = pre_back(
        expert_pre, batch_nt(cotangent_slot, expert_down), slot_gate
    )
    grad_shared_pre, shared_dots, shared_stat = pre_back(
        shared_pre, dot_nt(cotangent_full, shared_down), mix_gate
    )
    grad_buffer = batch_nt(grad_expert_pre, expert_in).astype(bf16).reshape(experts * CAP, width)
    grad_partial = (dot_nn(slots, grad_buffer) + dot_nt(grad_shared_pre, shared_in)).astype(bf16)
    grad_expert_in = batch_tn(buffer, grad_expert_pre).astype(bf16)
    grad_shared_in = dot_tn(normed_ffn, grad_shared_pre).astype(bf16)[None]

    told = []
    stat_sum = shared_stat
    for e in range(experts):
        terms = jnp.stack([*two_terms(expert_dots[e]), *two_terms(expert_stat[e])], axis=1)
        found = dot_nn(slots[:, e * CAP : (e + 1) * CAP], terms)
        told.append(found[:, 0] + found[:, 1])
        stat_sum = stat_sum + found[:, 2] + found[:, 3]
    told = all_of_col(jnp.stack([*told, shared_dots, stat_sum]), cols, col)
    grad_probs = told[:, :experts].reshape(EXPERTS, length).T
    grad_mix = jnp.sum(told[:, experts], axis=0)[:, None] * mix_gate * (1.0 - mix_gate)
    grad_logits = probs * (grad_probs - jnp.sum(probs * grad_probs, axis=1, keepdims=True))
    grad_small = jnp.concatenate([grad_logits, grad_mix], axis=1)
    ffn_stat = (
        jnp.sum(told[:, experts + 1], axis=0)[:, None] + jnp.sum(grad_small * logits, axis=1, keepdims=True)
    ) / inverse_ffn

    grad_ffn = line_scatter(grad_partial, cols, col) + dot_nt(
        grad_small.astype(bf16), mine(all_small, 0)
    )
    grad_gain_ffn = jnp.sum(grad_ffn * residual_mine * inverse_ffn, axis=0)
    grad_residual = (
        cotangent.astype(f32)
        + gain_ffn[None, :] * grad_ffn * inverse_ffn
        - residual_mine * (inverse_ffn**3 * ffn_stat / width)
    )
    grad_res_full = line_gather(grad_residual.astype(bf16), cols, col)

    out_mine = lax.dynamic_slice_in_dim(all_out, col * head_width, head_width, 0)
    grad_mixed = dot_nt(grad_res_full, out_mine).astype(bf16)
    grad_out = dot_tn(grad_res_full, mixed).astype(bf16)
    grad_heads, grad_bias = attend_back(heads_pre, cosine, sine, seg_col, seg_row, grad_mixed)
    normed_partial = dot_nt(grad_heads, all_heads).astype(bf16)
    weighed = normed_partial.astype(f32) * inputs_wide
    attn_stat = jnp.sum(all_of_col(jnp.sum(weighed * gains[0][None, :], axis=1)[None], cols, col), axis=0)
    grad_gain_attn = jnp.sum(weighed * inverse_attn, axis=0)
    grad_qkv = dot_tn(normed, grad_heads).astype(bf16)
    grad_attn = line_scatter(normed_partial, cols, col)
    inputs_mine = inputs.astype(f32)
    input_grad = (
        grad_residual
        + gain_attn[None, :] * grad_attn * inverse_attn
        - inputs_mine * (inverse_attn**3 * attn_stat.reshape(-1, 1) / width)
    )

    def scattered(values, axis):
        return lax.psum_scatter(values, "row", scatter_dimension=axis, tiled=True).astype(f32)

    if alike:
        down = scattered(jnp.concatenate([grad_expert_down, grad_shared_down], 0), 2)
        into = scattered(jnp.concatenate([grad_expert_in, grad_shared_in], 0), 1)
        grad_expert_down, grad_shared_down = down[:experts], down[experts]
        grad_expert_in, grad_shared_in = into[:experts], into[experts]
    else:
        grad_expert_down = scattered(grad_expert_down, 2)
        grad_shared_down = scattered(grad_shared_down, 2)[0]
        grad_expert_in = scattered(grad_expert_in, 1)
        grad_shared_in = scattered(grad_shared_in, 1)[0]
    attention = scattered(jnp.concatenate([grad_qkv, grad_out], 1), 0)
    grad_query, grad_key, grad_value = from_heads(attention[:, : 3 * head_width])
    grad_out = attention[:, 3 * head_width :].T

    grad_small_weights = lax.psum(dot_tn(grad_small.astype(bf16), normed_ffn), "row")
    grad_small_weights = lax.dynamic_slice_in_dim(grad_small_weights, row * depth, depth, 1)
    spread = jnp.zeros((4, width), f32)
    vectors = jnp.concatenate([grad_gain_ffn[None], jnp.stack(from_heads(grad_bias))[:, 0]], 0)
    spread = lax.dynamic_update_slice_in_dim(spread, vectors, col * part, 1)
    sums = mine(lax.psum(jnp.concatenate([grad_gain_attn[None], spread], 0), ("row", "col")))
    return (
        output,
        input_grad,
        sums[0],
        grad_query,
        grad_key,
        grad_value,
        sums[2],
        sums[3],
        sums[4],
        grad_out,
        sums[1],
        grad_small_weights[:EXPERTS].T,
        grad_expert_in[:, :, :hidden],
        grad_expert_in[:, :, hidden:],
        grad_expert_down,
        grad_shared_in[:, :hidden_shared],
        grad_shared_in[:, hidden_shared:],
        grad_shared_down,
        grad_small_weights[EXPERTS],
    )


def solution(mesh):
    in_specs = (
        P("row", "col"),
        P("row", None),
        P("row", None),
        P("col"),
        P("row", "col"),
        P("row", "col"),
        P("row", "col"),
        P("col"),
        P("col"),
        P("col"),
        P("col", "row"),
        P("col"),
        P("row", None),
        P("col", "row", None),
        P("col", "row", None),
        P("col", None, "row"),
        P("row", "col"),
        P("row", "col"),
        P("col", "row"),
        P("row"),
        P("row", "col"),
    )
    out_specs = (
        P("row", "col"),
        P("row", "col"),
        P("col"),
        P("row", "col"),
        P("row", "col"),
        P("row", "col"),
        P("col"),
        P("col"),
        P("col"),
        P("col", "row"),
        P("col"),
        P("row", None),
        P("col", "row", None),
        P("col", "row", None),
        P("col", None, "row"),
        P("row", "col"),
        P("row", "col"),
        P("col", "row"),
        P("row"),
    )
    body = functools.partial(local, mesh.shape["row"], mesh.shape["col"])
    return jax.shard_map(body, mesh=mesh, in_specs=in_specs, out_specs=out_specs, check_vma=False)
```

```python
import functools

import jax
import jax.numpy as jnp
from jax import lax
from jax.experimental import pallas as pl
from jax.experimental.pallas import tpu as pltpu
from jax.sharding import PartitionSpec as P

HEAD_DIM = 128
EXPERTS = 8
TOP = 4
CAP = 576
SPAN = 256

EPSILON = 1e-06
THETA = 1000000.0
NEGATIVE = -1e30

f32 = jnp.float32
bf16 = jnp.bfloat16


def dot_nn(left, right):
    return jnp.dot(left, right, preferred_element_type=f32)


def dot_nt(left, right):
    return lax.dot_general(left, right, (((1,), (1,)), ((), ())), preferred_element_type=f32)


def dot_tn(left, right):
    return lax.dot_general(left, right, (((0,), (0,)), ((), ())), preferred_element_type=f32)


def batch_nn(left, right):
    return jnp.einsum("ecd,edf->ecf", left, right, preferred_element_type=f32)


def batch_nt(left, right):
    return jnp.einsum("ecf,edf->ecd", left, right, preferred_element_type=f32)


def batch_tn(left, right):
    return jnp.einsum("ecd,ecf->edf", left, right, preferred_element_type=f32)


def after(values, *earlier):
    if not earlier:
        return values
    leaves, tree = jax.tree.flatten(values)
    anywhere = pl.BlockSpec(memory_space=pl.ANY)
    leaves = pl.pallas_call(
        lambda *refs: None,
        in_specs=[anywhere] * (len(leaves) + len(earlier)),
        out_specs=[anywhere] * len(leaves),
        out_shape=[jax.ShapeDtypeStruct(leaf.shape, leaf.dtype) for leaf in leaves],
        input_output_aliases={i: i for i in range(len(leaves))},
    )(*leaves, *earlier)
    return jax.tree.unflatten(tree, leaves)


class Gather:
    def __init__(self, block, count, me):
        self.block, self.count, self.me, self.hops = block, count, me, 0
        self.up = self.down = block
        full = jnp.zeros((block.shape[0], count * block.shape[1]), block.dtype)
        self.full = lax.dynamic_update_slice_in_dim(full, block, me * block.shape[1], 1)

    def place(self, piece, there, index):
        piece, index = jnp.where(there, piece, self.block), jnp.where(there, index, self.me)
        self.full = lax.dynamic_update_slice_in_dim(self.full, piece, index * self.block.shape[1], 1)

    def placed(self):
        if self.hops:
            self.place(self.up, self.me >= self.hops, self.me - self.hops)
            self.place(self.down, self.me + self.hops < self.count, self.me + self.hops)

    def hop(self, *earlier):
        if earlier:
            self.up, self.down = after((self.up, self.down), *earlier)
        self.up_before = self.up
        self.placed()
        done, count = self.hops, self.count
        self.up = lax.ppermute(self.up, "col", [(i, i + 1) for i in range(done, count - 1)])
        self.down = lax.ppermute(self.down, "col", [(i, i - 1) for i in range(1, count - done)])
        self.hops += 1

    def result(self):
        while self.hops < self.count - 1:
            self.hop()
        self.placed()
        return self.full


def hop_kernel(first, where, *refs):
    del where
    up_out, down_out = refs[-2:]
    if first:
        up_out[...], down_out[...] = refs[0][...], refs[1][...]
    else:
        up_out[...] = (refs[0][...].astype(f32) + refs[2][...].astype(f32)).astype(bf16)
        down_out[...] = (refs[1][...].astype(f32) + refs[3][...].astype(f32)).astype(bf16)


def hop_blocks(partial, width, where, sums, earlier):
    rows = partial.shape[0]
    tile = max(size for size in range(16, 257, 16) if rows % size == 0)
    plain = pl.BlockSpec((tile, width), lambda i, where: (i, 0))
    return pl.pallas_call(
        functools.partial(hop_kernel, not sums),
        grid_spec=pltpu.PrefetchScalarGridSpec(
            num_scalar_prefetch=1,
            grid=(rows // tile,),
            in_specs=[
                pl.BlockSpec((tile, width), lambda i, where: (i, where[0])),
                pl.BlockSpec((tile, width), lambda i, where: (i, where[1])),
                *[plain for _ in sums],
                *[pl.BlockSpec(memory_space=pl.ANY) for _ in earlier],
            ],
            out_specs=[plain, plain],
        ),
        out_shape=[jax.ShapeDtypeStruct((rows, width), bf16)] * 2,
        compiler_params=pltpu.CompilerParams(vmem_limit_bytes=16 << 20),
        cost_estimate=pl.CostEstimate(flops=2 * rows * width, bytes_accessed=12 * rows * width, transcendentals=0),
    )(where, partial, partial, *sums, *earlier)


class Scatter:
    def __init__(self, partial, count, me):
        self.partial, self.count, self.me, self.hops = partial, count, me, 0
        self.width = partial.shape[1] // count
        self.sums = ()

    def hop(self, *earlier):
        far = self.count - 1 - self.hops
        where = jnp.stack([jnp.minimum(self.me + far, self.count - 1), jnp.maximum(self.me - far, 0)])
        up, down = hop_blocks(self.partial, self.width, where.astype(jnp.int32), self.sums, earlier)
        self.sent = up
        up = lax.ppermute(up, "col", [(i, i + 1) for i in range(self.count - far)])
        down = lax.ppermute(down, "col", [(i, i - 1) for i in range(far, self.count)])
        self.sums = (up, down)
        self.hops += 1

    def result(self):
        while self.hops < self.count - 1:
            self.hop()
        own = lax.dynamic_slice_in_dim(self.partial, self.me * self.width, self.width, 1)
        return own.astype(f32) + self.sums[0].astype(f32) + self.sums[1].astype(f32)


def all_of_col(block, count, me):
    full = jnp.zeros((count,) + block.shape, block.dtype)
    full = lax.dynamic_update_slice_in_dim(full, block[None], me, 0)
    for step in range(1, count):
        got = lax.ppermute(block, "col", [(i, (i + step) % count) for i in range(count)])
        full = lax.dynamic_update_slice_in_dim(full, got[None], lax.rem(me + count - step, count), 0)
    return full


def spans(length):
    return [(max(0, first - SPAN), first, first + SPAN) for first in range(0, length, SPAN)]


def turned(values, cosine, sine):
    return values * cosine + pltpu.roll(values, HEAD_DIM // 2, 1) * sine


def turned_back(values, cosine, sine):
    return values * cosine - pltpu.roll(values, HEAD_DIM // 2, 1) * sine


def soft_weights(query, key, seg_col, seg_row, low, first, high):
    scores = dot_nt(query, key) * HEAD_DIM ** (-0.5)
    shape = (high - first, high - low)
    at_query = first + lax.broadcasted_iota(jnp.int32, shape, 0)
    at_key = low + lax.broadcasted_iota(jnp.int32, shape, 1)
    allowed = (at_key <= at_query) & (seg_col[first:high, :] == seg_row[:, low:high])
    scores = jnp.where(allowed, scores, NEGATIVE)
    weights = jnp.exp(scores - jnp.max(scores, axis=1, keepdims=True))
    return weights / jnp.sum(weights, axis=1, keepdims=True)


def attend_kernel(pre_q, pre_k, pre_v, bias, cosine, sine, seg_col, seg_row, mixed, query, key, value):
    length = pre_q.shape[0]
    query[...] = turned(pre_q[...] + bias[0:1, :], cosine[...], sine[...]).astype(bf16)
    key[...] = turned(pre_k[...] + bias[1:2, :], cosine[...], sine[...]).astype(bf16)
    value[...] = (pre_v[...] + bias[2:3, :]).astype(bf16)
    for low, first, high in spans(length):
        weights = soft_weights(query[first:high, :], key[low:high, :], seg_col, seg_row, low, first, high)
        mixed[first:high, :] = dot_nn(weights.astype(bf16), value[low:high, :]).astype(bf16)


def attend_back_kernel(
    query, key, value, cosine, sine, seg_col, seg_row, grad_mixed, grad_pre, grad_bias, key_sum, value_sum
):
    length = query.shape[0]
    scale = HEAD_DIM ** (-0.5)
    part = pl.program_id(1)

    @pl.when(part == 0)
    def _():
        key_sum[...] = jnp.zeros_like(key_sum)
        value_sum[...] = jnp.zeros_like(value_sum)
        query_bias = jnp.zeros((1, HEAD_DIM), f32)
        for low, first, high in spans(length):
            q, k, v = query[first:high, :], key[low:high, :], value[low:high, :]
            grad = grad_mixed[first:high, :]
            weights = soft_weights(q, k, seg_col, seg_row, low, first, high)
            grad_soft = dot_nt(grad, v)
            inner = jnp.sum(weights * grad_soft, axis=1, keepdims=True)
            grad_scores = (weights * (grad_soft - inner)).astype(bf16)
            grad_query = dot_nn(grad_scores, k) * scale
            grad_query = turned_back(grad_query, cosine[first:high, :], sine[first:high, :]).astype(bf16)
            grad_pre[first:high, :] = grad_query
            query_bias += jnp.sum(grad_query.astype(f32), axis=0, keepdims=True)
            key_sum[low:high, :] += dot_tn(grad_scores, q) * scale
            value_sum[low:high, :] += dot_tn(weights.astype(bf16), grad)
        grad_bias[0:1, :] = query_bias

    @pl.when(part == 1)
    def _():
        grad_key = turned_back(key_sum[...], cosine[...], sine[...]).astype(bf16)
        grad_pre[...] = grad_key
        grad_bias[1:2, :] = jnp.sum(grad_key.astype(f32), axis=0, keepdims=True)

    @pl.when(part == 2)
    def _():
        grad_value = value_sum[...].astype(bf16)
        grad_pre[...] = grad_value
        grad_bias[2:3, :] = jnp.sum(grad_value.astype(f32), axis=0, keepdims=True)


def head_spec(rows, skip=0):
    return pl.BlockSpec((rows, HEAD_DIM), lambda h, *_: (0, skip + h))


def whole_spec(array):
    return pl.BlockSpec(array.shape, lambda *_: (0, 0))


def attend(pre, bias, cosine, sine, seg_col, seg_row):
    length, width = pre.shape[0], pre.shape[1] // 3
    heads = width // HEAD_DIM
    tables = (cosine, sine, seg_col, seg_row)
    return pl.pallas_call(
        attend_kernel,
        grid=(heads,),
        in_specs=[
            head_spec(length),
            head_spec(length, heads),
            head_spec(length, 2 * heads),
            head_spec(3),
            *[whole_spec(table) for table in tables],
        ],
        out_specs=[head_spec(length)] * 4,
        out_shape=[jax.ShapeDtypeStruct((length, width), bf16)] * 4,
        compiler_params=pltpu.CompilerParams(vmem_limit_bytes=32 << 20),
        cost_estimate=pl.CostEstimate(
            flops=width * length * 2 * SPAN * 4, bytes_accessed=20 * length * width, transcendentals=0
        ),
    )(pre, pre, pre, bias, *tables)


def attend_back(query, key, value, cosine, sine, seg_col, seg_row, grad_mixed):
    length, width = query.shape
    heads = width // HEAD_DIM
    tables = (cosine, sine, seg_col, seg_row)
    return pl.pallas_call(
        attend_back_kernel,
        grid=(heads, 3),
        in_specs=[
            *[head_spec(length)] * 3,
            *[whole_spec(table) for table in tables],
            head_spec(length),
        ],
        out_specs=[pl.BlockSpec((length, HEAD_DIM), lambda h, part: (0, part * heads + h)), head_spec(3)],
        out_shape=[
            jax.ShapeDtypeStruct((length, 3 * width), bf16),
            jax.ShapeDtypeStruct((3, width), f32),
        ],
        scratch_shapes=[pltpu.VMEM((length, HEAD_DIM), f32), pltpu.VMEM((length, HEAD_DIM), f32)],
        compiler_params=pltpu.CompilerParams(vmem_limit_bytes=32 << 20),
        cost_estimate=pl.CostEstimate(
            flops=width * length * 2 * SPAN * 10, bytes_accessed=14 * length * width, transcendentals=0
        ),
    )(query, key, value, *tables, grad_mixed)


def tile_of(size, most):
    return max(tile for tile in range(128, most + 1, 128) if size % tile == 0)


def batch_nt_kernel(left, right, *refs):
    refs[-1][0] = dot_nt(left[0], right[0]).astype(bf16)


def batch_nt_tiles(left, right, *earlier):
    count, rows, depth = left.shape
    columns = right.shape[1]
    tile = tile_of(columns, 512)
    return pl.pallas_call(
        batch_nt_kernel,
        grid=(count, columns // tile),
        in_specs=[
            pl.BlockSpec((1, rows, depth), lambda e, n: (e, 0, 0)),
            pl.BlockSpec((1, tile, depth), lambda e, n: (e, n, 0)),
            *[pl.BlockSpec(memory_space=pl.ANY) for _ in earlier],
        ],
        out_specs=pl.BlockSpec((1, rows, tile), lambda e, n: (e, 0, n)),
        out_shape=jax.ShapeDtypeStruct((count, rows, columns), bf16),
        compiler_params=pltpu.CompilerParams(vmem_limit_bytes=56 << 20),
        cost_estimate=pl.CostEstimate(
            flops=2 * count * rows * depth * columns,
            bytes_accessed=2 * count * (rows * depth + depth * columns + rows * columns),
            transcendentals=0,
        ),
    )(left, right, *earlier)


def two_products_kernel(turn, slots, routed, left, right, *refs):
    dot = dot_nt if turn else dot_nn
    refs[-1][...] = (dot_nn(slots[...], routed[...]) + dot(left[...], right[0])).astype(bf16)


def two_products(slots, routed, left, right, turn, *earlier):
    length, depth = slots.shape
    last = right.shape[0] - 1
    inner, columns = left.shape[1], routed.shape[1]
    tile = tile_of(columns, 256)
    return pl.pallas_call(
        functools.partial(two_products_kernel, turn),
        grid=(columns // tile,),
        in_specs=[
            pl.BlockSpec((length, depth), lambda n: (0, 0)),
            pl.BlockSpec((depth, tile), lambda n: (0, n)),
            pl.BlockSpec((length, inner), lambda n: (0, 0)),
            pl.BlockSpec((1, tile, inner), lambda n: (last, n, 0))
            if turn
            else pl.BlockSpec((1, inner, tile), lambda n: (last, 0, n)),
            *[pl.BlockSpec(memory_space=pl.ANY) for _ in earlier],
        ],
        out_specs=pl.BlockSpec((length, tile), lambda n: (0, n)),
        out_shape=jax.ShapeDtypeStruct((length, columns), bf16),
        compiler_params=pltpu.CompilerParams(vmem_limit_bytes=56 << 20),
        cost_estimate=pl.CostEstimate(
            flops=2 * length * columns * (depth + inner),
            bytes_accessed=2 * (length + columns) * (depth + inner),
            transcendentals=0,
        ),
    )(slots, routed, left, right, *earlier)


def rotary_tables(length):
    position = jnp.arange(length).astype(f32)
    exponent = jnp.arange(HEAD_DIM // 2).astype(f32) * (2.0 / HEAD_DIM)
    angles = position[:, None] * jnp.exp(-exponent * jnp.log(THETA))[None, :]
    cosine, sine = jnp.cos(angles), jnp.sin(angles)
    return jnp.concatenate([cosine, cosine], 1), jnp.concatenate([-sine, sine], 1)


def two_terms(values):
    high = values.astype(bf16)
    return high, (values - high.astype(f32)).astype(bf16)


def unwritten(shape, dtype):
    return pl.pallas_call(
        lambda out: None,
        out_specs=pl.BlockSpec(memory_space=pl.ANY),
        out_shape=jax.ShapeDtypeStruct(shape, dtype),
    )()


def stacked(first, last):
    count = first.shape[0]
    both = unwritten((count + last.shape[0],) + first.shape[1:], first.dtype)
    both = lax.dynamic_update_slice_in_dim(both, first, 0, 0)
    return lax.dynamic_update_slice_in_dim(both, last, count, 0)


def beside(parts):
    whole = unwritten((parts[0].shape[0], sum(part.shape[1] for part in parts)), bf16)
    start = 0
    for part in parts:
        whole = lax.dynamic_update_slice_in_dim(whole, part.astype(bf16), start, 1)
        start += part.shape[1]
    return whole


def local(
    rows,
    cols,
    inputs,
    segments,
    routes,
    gain_attn,
    w_query,
    w_key,
    w_value,
    b_query,
    b_key,
    b_value,
    w_out,
    gain_ffn,
    w_router,
    w_expert_gate,
    w_expert_up,
    w_expert_down,
    w_shared_gate,
    w_shared_up,
    w_shared_down,
    w_shared_mix,
    cotangent,
):
    length, part = inputs.shape
    width = part * cols
    experts, depth, hidden = w_expert_gate.shape
    hidden_shared = w_shared_gate.shape[1]
    head_width = w_query.shape[1]
    alike = hidden == hidden_shared
    col = lax.axis_index("col")

    def mine(array, axis=1):
        return lax.dynamic_slice_in_dim(array, col * part, part, axis)

    gain_rows = jnp.stack([*two_terms(gain_attn), *two_terms(gain_ffn)])
    riders = jnp.concatenate([gain_rows, jnp.zeros((12, part), bf16)], 0)
    inputs_gather = Gather(jnp.concatenate([inputs, riders], 0), cols, col)
    inputs_gather.hop()
    first_hop = inputs_gather.up, inputs_gather.down
    inputs_full = inputs_gather.result()
    gain_rows = inputs_full[length : length + 4].astype(f32)
    full_gain_attn = gain_rows[0:1] + gain_rows[1:2]
    full_gain_ffn = gain_rows[2:3] + gain_rows[3:4]

    all_heads = lax.all_gather(jnp.concatenate([w_query, w_key, w_value], 1), "row", axis=0, tiled=True)
    small_rows = jnp.concatenate([w_router.T, w_shared_mix[None], jnp.zeros((7, depth), bf16)], 0)
    expert_in = jnp.concatenate([w_expert_gate, w_expert_up], axis=2)
    shared_in = jnp.concatenate([w_shared_gate, w_shared_up], axis=1)[None]
    shared_down = w_shared_down[None]
    if alike:
        all_in = lax.all_gather(jnp.concatenate([expert_in, shared_in], 0), "row", axis=1, tiled=True)
        all_in = [all_in, all_in]
    else:
        all_in = [lax.all_gather(part, "row", axis=1, tiled=True) for part in (expert_in, shared_in)]
    out_rows = unwritten((width + small_rows.shape[0], depth), bf16)
    out_rows = lax.dynamic_update_slice_in_dim(out_rows, small_rows, width, 0)
    out_block = after(w_out, *first_hop)
    out_rows = lax.dynamic_update_slice_in_dim(out_rows, out_block, col * head_width, 0)
    for step in range(1, cols):
        got = lax.ppermute(out_block, "col", [(i, (i + step) % cols) for i in range(cols)])
        out_rows = lax.dynamic_update_slice_in_dim(out_rows, got, lax.rem(col + cols - step, cols) * head_width, 0)
    all_out = lax.all_gather(out_rows, "row", axis=1, tiled=True)
    all_small = all_out[width:]

    named = jnp.any(routes[:, :, None] == jnp.arange(EXPERTS)[None, None, :], axis=1)
    at = jnp.arange(length)
    earlier = (at[None, :] < at[:, None]).astype(bf16)
    place = dot_nn(earlier, named.astype(bf16))
    kept = named & (place < CAP)
    place_here = lax.dynamic_slice_in_dim(jnp.where(kept, place, -1.0), col * experts, experts, 1)
    slots = (place_here[:, :, None] == jnp.arange(CAP).astype(f32)[None, None, :]).astype(bf16)
    slots = slots.reshape(length, experts * CAP)

    cosine, sine = rotary_tables(length)
    seg_row = segments
    seg_col = segments.T

    inputs_wide = inputs_full[:length].astype(f32)
    inverse_attn = lax.rsqrt(jnp.mean(inputs_wide * inputs_wide, axis=1, keepdims=True) + EPSILON)
    normed = (inputs_wide * inverse_attn * full_gain_attn).astype(bf16)
    bias = jnp.stack([b_query, b_key, b_value])
    mixed, *heads = attend(dot_nn(normed, all_heads), bias, cosine, sine, seg_col, seg_row)
    mixed_full = Gather(mixed, cols, col).result()
    cotangent_gather = Gather(after(cotangent, mixed_full), cols, col)
    cotangent_gather.hop()
    if alike:
        all_down = [jnp.concatenate([w_expert_down, shared_down], 0)]
    else:
        all_down = [w_expert_down, shared_down]
    all_down = [lax.all_gather(after(part, mixed), "row", axis=2, tiled=True) for part in all_down]
    residual = inputs_wide + dot_nn(mixed_full, all_out[:width])
    inverse_ffn = lax.rsqrt(jnp.mean(residual * residual, axis=1, keepdims=True) + EPSILON)
    normed_ffn = (residual * inverse_ffn * full_gain_ffn).astype(bf16)
    residual_mine = mine(residual)
    cotangent_gather.hop(normed_ffn)

    logits = dot_nt(normed_ffn, all_small)[:, : EXPERTS + 1]
    probs = jax.nn.softmax(logits[:, :EXPERTS], axis=-1)
    mix_gate = jax.nn.sigmoid(logits[:, EXPERTS:])
    probs_here = lax.dynamic_slice_in_dim(probs, col * experts, experts, 1)
    slot_gates = sum(dot_tn(slots, term) for term in two_terms(probs_here))
    slot_gate = jnp.concatenate(
        [slot_gates[e * CAP : (e + 1) * CAP, e : e + 1][None] for e in range(experts)], axis=0
    )

    buffer = dot_tn(slots, normed_ffn).astype(bf16).reshape(experts, CAP, width)
    expert_pre = batch_nn(buffer, all_in[0][:experts]).astype(bf16)
    shared_pre = dot_nn(normed_ffn, all_in[1][-1]).astype(bf16)

    def halves(pre):
        half = pre.shape[-1] // 2
        return pre[..., :half].astype(f32), pre[..., half:].astype(f32)

    def activated(pre, scale):
        gate, up = halves(pre)
        return (gate * jax.nn.sigmoid(gate) * up * scale).astype(bf16)

    cotangent_gather.hop(expert_pre)
    cotangent_full = after(cotangent_gather.result(), shared_pre)
    expert_act = activated(expert_pre, slot_gate)
    shared_act = activated(shared_pre, mix_gate)
    cotangent_slot = dot_tn(slots, cotangent_full).astype(bf16).reshape(experts, CAP, width)
    grad_expert_down = batch_tn(expert_act, cotangent_slot).astype(bf16)
    grad_shared_down = dot_tn(shared_act, cotangent_full).astype(bf16)[None]
    if alike:
        grad_downs = [(stacked(grad_expert_down, grad_shared_down), 2)]
    else:
        grad_downs = [(grad_expert_down, 2), (grad_shared_down, 2)]
    all_down = [after(part, *[grad for grad, _ in grad_downs]) for part in all_down]
    expert_down, shared_down = all_down[0][:experts], all_down[-1][-1]

    def pre_back(pre, grad_act, scale):
        gate, up = halves(pre)
        sigmoid = jax.nn.sigmoid(gate)
        silu = gate * sigmoid
        dots = jnp.sum(silu * up * grad_act, axis=-1)
        scaled = grad_act * scale
        grad_gate = scaled * up * sigmoid * (1.0 + gate * (1.0 - sigmoid))
        grad_up = scaled * silu
        stat = jnp.sum(grad_gate * gate + grad_up * up, axis=-1)
        return jnp.concatenate([grad_gate.astype(bf16), grad_up.astype(bf16)], axis=-1), dots, stat

    grad_expert_pre, expert_dots, expert_stat = pre_back(
        expert_pre, batch_nt(cotangent_slot, expert_down), slot_gate
    )
    grad_shared_pre, shared_dots, shared_stat = pre_back(
        shared_pre, dot_nt(cotangent_full, shared_down), mix_gate
    )
    told = []
    stat_sum = shared_stat
    for e in range(experts):
        terms = jnp.stack([*two_terms(expert_dots[e]), *two_terms(expert_stat[e])], axis=1)
        found = dot_nn(slots[:, e * CAP : (e + 1) * CAP], terms)
        told.append(found[:, 0] + found[:, 1])
        stat_sum = stat_sum + found[:, 2] + found[:, 3]
    told_here = jnp.stack([*told, shared_dots, stat_sum])

    told = all_of_col(told_here, cols, col)
    grad_buffer = batch_nt_tiles(grad_expert_pre, all_in[0], told_here).reshape(experts * CAP, width)
    grad_partial = two_products(slots, grad_buffer, grad_shared_pre, all_in[1], True, told)

    scatter = Scatter(grad_partial, cols, col)
    scatter.hop()
    grad_expert_in = batch_tn(buffer, after(grad_expert_pre, grad_partial)).astype(bf16)
    scatter.hop(grad_expert_in)
    grad_shared_in = dot_tn(normed_ffn, after(grad_shared_pre, grad_partial, grad_expert_in)).astype(bf16)[None]
    if alike:
        grad_ins = [(stacked(grad_expert_in, grad_shared_in), 1)]
    else:
        grad_ins = [(grad_expert_in, 1), (grad_shared_in, 1)]
    scatter.hop(grad_ins[-1][0])
    expert_out = batch_nn(after(expert_act, scatter.sent), expert_down).astype(bf16).reshape(experts * CAP, width)
    sums_mark = scatter.sent
    grad_probs = told[:, :experts].reshape(EXPERTS, length).T
    grad_mix = jnp.sum(told[:, experts], axis=0)[:, None] * mix_gate * (1.0 - mix_gate)
    grad_logits = probs * (grad_probs - jnp.sum(probs * grad_probs, axis=1, keepdims=True))
    grad_small = jnp.concatenate([grad_logits, grad_mix], axis=1)
    ffn_stat = (
        jnp.sum(told[:, experts + 1], axis=0)[:, None] + jnp.sum(grad_small * logits, axis=1, keepdims=True)
    ) / inverse_ffn

    grad_ffn = scatter.result() + dot_nt(grad_small.astype(bf16), mine(all_small, 1)[: EXPERTS + 1].T)
    grad_gain_ffn = jnp.sum(grad_ffn * residual_mine * inverse_ffn, axis=0)
    grad_residual = (
        cotangent.astype(f32)
        + gain_ffn[None, :] * grad_ffn * inverse_ffn
        - residual_mine * (inverse_ffn**3 * ffn_stat / width)
    )

    def scattered(grads):
        return [lax.psum_scatter(grad, "row", scatter_dimension=axis, tiled=True) for grad, axis in grads]

    downs = scattered(grad_downs)
    ins = scattered([(after(grad, downs[-1], sums_mark), axis) for grad, axis in grad_ins])
    grad_expert_down, grad_shared_down = (downs[0][:experts], downs[0][experts]) if alike else (downs[0], downs[1][0])
    grad_expert_down, grad_shared_down = grad_expert_down.astype(f32), grad_shared_down.astype(f32)

    gather = Gather(after(grad_residual.astype(bf16), expert_out), cols, col)
    gather.hop()
    ffn_partial = two_products(slots, expert_out, shared_act, all_down[-1], False, grad_residual)
    scatter = Scatter(ffn_partial, cols, col)
    gather.hop(ffn_partial)
    scatter.hop(gather.up_before)
    while gather.hops < cols - 1:
        gather.hop(*scatter.sums)
        scatter.hop(gather.up_before)
    grad_res_full = after(gather.result(), *scatter.sums)
    output = residual_mine + scatter.result()
    out_sums = scatter.sums

    out_mine = lax.dynamic_slice_in_dim(all_out, col * head_width, head_width, 0)
    grad_mixed = dot_nt(grad_res_full, out_mine).astype(bf16)
    grad_heads, grad_bias = attend_back(*heads, cosine, sine, seg_col, seg_row, grad_mixed)
    grad_heads = after(grad_heads, *out_sums)
    normed_partial = dot_nt(grad_heads, all_heads)
    attn_stat = jnp.sum(normed_partial * inputs_wide * full_gain_attn, axis=1)
    stat_rows = attn_stat.astype(bf16).reshape(-1, part)
    stat_rows = jnp.concatenate([stat_rows, jnp.zeros((16 - length // part % 16, part), bf16)], 0)
    normed_partial = normed_partial.astype(bf16)
    ridden = unwritten((length + stat_rows.shape[0], width), bf16)
    ridden = lax.dynamic_update_slice_in_dim(ridden, normed_partial, 0, 0)
    ridden = lax.dynamic_update_slice_in_dim(ridden, jnp.tile(stat_rows, (1, cols)), length, 0)
    scatter = Scatter(ridden, cols, col)
    scatter.hop(output)
    late_heads = after(grad_heads, ridden)
    small_columns = dot_tn(normed_ffn, grad_small.astype(bf16))
    small_columns = jnp.concatenate([small_columns, jnp.zeros((width, 119), f32)], 1)
    attention = beside(
        [dot_tn(normed, late_heads), dot_tn(grad_res_full, mixed), small_columns]
    )
    scatter.hop(attention, grad_expert_down, grad_shared_down)
    attention_mark = scatter.sent
    grad_attn = scatter.result()
    attn_stat = grad_attn[length : length + length // part].reshape(-1, 1)
    grad_attn = grad_attn[:length]
    grad_gain_attn = jnp.sum(grad_attn * inputs.astype(f32) * inverse_attn, axis=0)
    input_grad = (
        grad_residual
        + gain_attn[None, :] * grad_attn * inverse_attn
        - inputs.astype(f32) * (inverse_attn**3 * attn_stat / width)
    )

    if alike:
        grad_expert_in, grad_shared_in = ins[0][:experts], ins[0][experts]
    else:
        grad_expert_in, grad_shared_in = ins[0], ins[1][0]
    grad_expert_in, grad_shared_in = grad_expert_in.astype(f32), grad_shared_in.astype(f32)
    [attention] = scattered([(after(attention, ins[-1], attention_mark), 0)])
    attention = attention.astype(f32)
    grad_query, grad_key, grad_value, grad_out = [
        attention[:, i * head_width : (i + 1) * head_width] for i in range(4)
    ]
    grad_out = grad_out.T
    grad_small = attention[:, 4 * head_width :]

    vectors = jnp.concatenate([grad_gain_attn[None], grad_gain_ffn[None], grad_bias], 0)
    sums = lax.psum(vectors, "row")
    return (
        output,
        input_grad,
        sums[0],
        grad_query,
        grad_key,
        grad_value,
        sums[2],
        sums[3],
        sums[4],
        grad_out,
        sums[1],
        grad_small[:, :EXPERTS],
        grad_expert_in[:, :, :hidden],
        grad_expert_in[:, :, hidden:],
        grad_expert_down,
        grad_shared_in[:, :hidden_shared],
        grad_shared_in[:, hidden_shared:],
        grad_shared_down,
        grad_small[:, EXPERTS],
    )


def solution(mesh):
    in_specs = (
        P("row", "col"),
        P("row", None),
        P("row", None),
        P("col"),
        P("row", "col"),
        P("row", "col"),
        P("row", "col"),
        P("col"),
        P("col"),
        P("col"),
        P("col", "row"),
        P("col"),
        P("row", None),
        P("col", "row", None),
        P("col", "row", None),
        P("col", None, "row"),
        P("row", "col"),
        P("row", "col"),
        P("col", "row"),
        P("row"),
        P("row", "col"),
    )
    out_specs = (
        P("row", "col"),
        P("row", "col"),
        P("col"),
        P("row", "col"),
        P("row", "col"),
        P("row", "col"),
        P("col"),
        P("col"),
        P("col"),
        P("col", "row"),
        P("col"),
        P("row", None),
        P("col", "row", None),
        P("col", "row", None),
        P("col", None, "row"),
        P("row", "col"),
        P("row", "col"),
        P("col", "row"),
        P("row"),
    )
    body = functools.partial(local, mesh.shape["row"], mesh.shape["col"])
    return jax.shard_map(body, mesh=mesh, in_specs=in_specs, out_specs=out_specs, check_vma=False)
```
